32 devices in a mesh: group: 2 (over y), inline: 4 (over z), xline: 4 (over x, core).
Axes of the slice: x: 2, y: 2, z: 4, core: 2. Of those that a mesh axis runs over, the one named last changes fastest.
Arguments:
- volume: bfloat16 [32, 64, 64, 128], P(('group', 'inline'), 'xline'), parts along dimension 0, may hold values from -6 to 6
- first_kernel: bfloat16 [27, 128, 128], P(None, 'xline'), may hold values from -0.109375 to 0.109375
- second_kernel: bfloat16 [27, 128, 128], P(None, 'xline'), may hold values from -0.109375 to 0.109375
- cotangent: bfloat16 [16, 32, 32, 128], P(('group', 'inline'), 'xline'), parts along dimension 0, may hold values from -0.15625 to 0.15625
Outputs:
- latent: bfloat16 [16, 32, 32, 128], P(('group', 'inline'), 'xline'), parts along dimension 0
- first_grad: float32 [884736], P(('group', 'inline', 'xline')), parts along dimension 0
- second_grad: float32 [884736], P(('group', 'inline', 'xline')), parts along dimension 0
The draws below stay inside these ranges and needn't reach their ends.
There are 2 independent parts, one for each index of `group`. The reference program is written for one: setup_inputs(seed, part) draws one part's arguments, and reference() takes and returns one part's arrays. A program takes and returns all parts, laid end to end along the dimension named above; an argument that names none is the same for every part. Nothing has to cross between parts.
All inputs are finite; a program needn't handle non-finite values.
Results may differ from the reference program's by a relative error of at most 0.0049.
Values may be sent and summed in bfloat16 or wider, within the bound.
A program may use at most 64 MiB of HBM per device.

```python
import jax
import jax.numpy as jnp
from jax import lax

CH = 128
KVOL = 27
XDEV = 4
YDEV = 16
ZD = 64
NX = 16
NY = 64
N_INLINE = 4
N_XLINE = 4


def strengthened(entries, rng, source, target, parts, factor):
    owner, partner = [(jnp.arange(entries.shape[position]) // (entries.shape[position] // parts)).reshape([-1 if axis == position else 1 for axis in range(entries.ndim)]) for position in (source, target)]
    chosen = jax.random.permutation(rng, parts)[partner]
    strong = (owner == chosen) | (owner == (partner + parts // 2) % parts)
    return jnp.where(strong, factor * entries, entries)


def shard_levels(stream_key, extent, pieces, least, high):
    def one(dim, blocks):
        draws = jax.random.uniform(jax.random.fold_in(jax.random.fold_in(stream_key, 6), dim), (blocks,), jnp.float32, least / len(pieces), high / len(pieces))
        return jnp.repeat(jnp.exp(draws), extent[dim] // blocks).reshape((-1,) + (1,) * (len(extent) - dim - 1))

    level = one(*pieces[0])
    for cut in pieces[1:]:
        level = level * one(*cut)
    return level


def bell_draw(key, extent, deviation, most, pieces=(), held_as=jnp.bfloat16):
    drawn = jax.random.normal(key, extent, jnp.float32) * deviation
    if len(pieces) > 0:
        drawn = shard_levels(key, extent, pieces, -0.22, 0.18) * drawn
    return jnp.clip(drawn, min=-most, max=most).astype(held_as)


def heavy_noise(key, dims, width, bound, split, heavy, kind=jnp.bfloat16):
    result = width * jax.random.normal(key, dims, jnp.float32)
    if split:
        result = result * shard_levels(key, dims, split, -0.22, 0.18)
    return jnp.clip(strengthened(result, jax.random.fold_in(key, 3), *heavy), -bound, bound).astype(kind)


def setup_inputs(seed: int = 0, part: int = 0) -> dict:
    streams_of = jax.random.split(jax.random.key(seed), 5)
    part_splits = jax.random.split(jax.random.fold_in(streams_of[4], part), 5)
    volume = heavy_noise(part_splits[0], (NX, NY, ZD, CH), 1.0, 6.0, ((0, 4), (1, 4)), (0, 3, 4, 2.0))
    first_kernel = bell_draw(streams_of[1], (KVOL, CH, CH), (KVOL * CH) ** -0.5, 0.109375, ((1, 4),))
    second_kernel = bell_draw(streams_of[2], (KVOL, CH, CH), (KVOL * CH) ** -0.5, 0.109375, ((1, 4),))
    cotangent = bell_draw(part_splits[3], (NX // 2, NY // 2, ZD // 2, CH), ((XDEV * YDEV * ZD * N_INLINE * N_XLINE // 8) ** -0.5), 0.15625, ((0, 4), (1, 4)))
    return dict(volume=volume, first_kernel=first_kernel, second_kernel=second_kernel, cotangent=cotangent)


def split_tap(index):
    return index // 9, (index // 3) % 3, index % 3


def reference(volume, first_kernel, second_kernel, cotangent):
    rows = cotangent.shape[0]
    cols = cotangent.shape[1]
    depth = cotangent.shape[2]
    channels = volume.shape[3]
    count = rows * cols * depth
    fine_pad = jnp.pad(volume, ((1, 0), (1, 0), (1, 0), (0, 0)))

    def fine_slice(index):
        first, second, third = split_tap(index)
        piece = lax.slice(fine_pad, (first, second, third, 0),
                          (first + 2 * rows - 1, second + 2 * cols - 1, third + 2 * depth - 1, channels),
                          (2, 2, 2, 1))
        return piece.reshape(count, channels)

    pre_first = jnp.zeros((count, channels), jnp.float32)
    for index in range(27):
        pre_first = pre_first + jnp.dot(fine_slice(index), first_kernel[index], preferred_element_type=jnp.float32)
    hidden = jax.nn.silu(pre_first).astype(jnp.bfloat16).reshape(rows, cols, depth, channels)
    hidden_pad = jnp.pad(hidden, ((1, 1), (1, 1), (1, 1), (0, 0)))
    cot_pad = jnp.pad(cotangent, ((1, 1), (1, 1), (1, 1), (0, 0)))
    cot_flat = cotangent.reshape(count, channels)
    latent = jnp.zeros((count, channels), jnp.float32)
    back_hidden = jnp.zeros((count, channels), jnp.float32)
    second_parts = []
    for index in range(27):
        first, second, third = split_tap(index)
        piece = hidden_pad[first:first + rows, second:second + cols, third:third + depth].reshape(count, channels)
        latent = latent + jnp.dot(piece, second_kernel[index], preferred_element_type=jnp.float32)
        second_parts.append(jnp.dot(piece.T, cot_flat, preferred_element_type=jnp.float32))
        back_piece = cot_pad[2 - first:2 - first + rows, 2 - second:2 - second + cols,
                             2 - third:2 - third + depth].reshape(count, channels)
        back_hidden = back_hidden + jnp.dot(back_piece, second_kernel[index].T, preferred_element_type=jnp.float32)
    sigma = jax.nn.sigmoid(pre_first)
    back_pre = (back_hidden * sigma * (1.0 + pre_first * (1.0 - sigma))).astype(jnp.bfloat16)
    first_parts = []
    for index in range(27):
        first_parts.append(jnp.dot(fine_slice(index).T, back_pre, preferred_element_type=jnp.float32))
    latent = latent.astype(jnp.bfloat16).reshape(rows, cols, depth, channels)
    first_grad = jnp.stack(first_parts).reshape(-1)
    second_grad = jnp.stack(second_parts).reshape(-1)
    return (latent, first_grad, second_grad)
```

```python
import functools
import itertools

import jax
import jax.numpy as jnp
from jax import lax
from jax.experimental import pallas as pl
from jax.experimental.pallas import tpu as pltpu
from jax.sharding import PartitionSpec as P

F32 = jnp.float32
BF16 = jnp.bfloat16
MESH = pl.DeviceIdType.MESH
TAPS = 27
LANES = 128
ALL_WAYS = [d for d in itertools.product((-1, 0, 1), repeat=2) if d != (0, 0)]
UP_WAYS = [(1, 0), (0, 1), (1, 1)]


def dot(left, right, dims=((1,), (0,))):
    return lax.dot_general(left, right, (dims, ((), ())), preferred_element_type=F32)


def remote(src, dst, send, recv, device):
    return pltpu.make_async_remote_copy(
        src_ref=src, dst_ref=dst, send_sem=send, recv_sem=recv,
        device_id=device, device_id_type=MESH,
    )


class Rim:
    def __init__(self, own, padded, low, send, recv, ways, place):
        inline, xline, inlines, xlines = place
        rows, cols = own.shape[0], own.shape[1]
        self.padded = padded
        self.items = []
        for n, (di, dx) in enumerate(ways):
            def there(si, sx, place=place):
                ok = None
                for step, at, count in ((si, inline, inlines), (sx, xline, xlines)):
                    if step == 1:
                        one = at < count - 1
                    elif step == -1:
                        one = at > 0
                    else:
                        continue
                    ok = one if ok is None else jnp.logical_and(ok, one)
                return ok

            def source(step, count):
                return {1: pl.ds(count - 1, 1), -1: pl.ds(0, 1), 0: pl.ds(0, count)}[step]

            def target(step, count):
                return {1: pl.ds(0, 1), -1: pl.ds(low + count, 1), 0: pl.ds(low, count)}[step]

            spot = (target(di, rows), target(dx, cols))
            copy = remote(
                own.at[source(di, rows), source(dx, cols)],
                padded.at[spot[0], spot[1]],
                send.at[n],
                recv.at[n],
                {
                    "inline": lax.rem(inline + di + inlines, inlines),
                    "xline": lax.rem(xline + dx + xlines, xlines),
                },
            )
            self.items.append((copy, spot, there(di, dx), there(-di, -dx)))

    def start(self):
        for copy, _, sends, _ in self.items:
            pl.when(sends)(copy.start)

    def clear(self):
        for _, spot, _, gets in self.items:
            @pl.when(jnp.logical_not(gets))
            def _():
                shape = (spot[0].size, spot[1].size) + tuple(self.padded.shape[2:])
                self.padded[spot[0], spot[1]] = jnp.zeros(shape, self.padded.dtype)

    def arrive(self):
        for copy, _, _, gets in self.items:
            pl.when(gets)(copy.wait_recv)

    def sent(self):
        for copy, _, sends, _ in self.items:
            pl.when(sends)(copy.wait_send)


class Spread:
    def __init__(self, shard, whole, sems, place):
        _, xline, _, _ = place
        send, recv, local = sems
        width = shard.shape[1]
        near = xline + 1 - 2 * lax.rem(xline, 2)
        far = lax.rem(xline + 2, 4)

        def part(index):
            return whole.at[:, pl.ds(pl.multiple_of(index * width, width), width), :]

        self.own = pltpu.make_async_copy(shard, part(xline), local)
        self.far = remote(shard, part(xline), send.at[0], recv.at[0], {"xline": far})
        self.near = remote(shard, part(xline), send.at[1], recv.at[1], {"xline": near})
        self.pass_on = remote(part(far), part(far), send.at[2], recv.at[2], {"xline": near})

    def start(self):
        self.far.start()
        self.near.start()
        self.own.start()

    def forward(self):
        self.far.wait_recv()
        self.pass_on.start()

    def arrive(self):
        self.own.wait()
        self.near.wait_recv()
        self.pass_on.wait_recv()

    def sent(self):
        self.far.wait_send()
        self.near.wait_send()
        self.pass_on.wait_send()


class Scatter:
    def __init__(self, total, bufs, sems, place):
        inline, xline, inlines, _ = place
        self.total, self.place = total, place
        self.p, self.r1, self.q, self.r2, self.s, self.r3 = bufs
        send, recv = sems
        self.core, self.x = lax.rem(xline, 2), xline // 2
        near = xline + 1 - 2 * self.core
        far = lax.rem(xline + 2, 4)
        self.rows = TAPS * LANES // (4 * inlines)
        self.one = remote(self.p.at[1 - self.core], self.r1, send.at[0], recv.at[0], {"xline": near})
        self.two = remote(self.q.at[1 - self.x], self.r2, send.at[1], recv.at[1], {"xline": far})
        self.three = []
        for d in range(1, inlines):
            to = lax.rem(inline + d, inlines)
            self.three.append(
                remote(self.s.at[to], self.r3.at[d - 1], send.at[1 + d], recv.at[1 + d], {"inline": to})
            )

    def first(self):
        slot_rows = self.p.shape[3]
        for slot in range(4 * self.place[2]):
            self.p[slot % 2, slot // 2 % 2, slot // 4] = self.total[
                pl.ds(slot * self.rows, slot_rows), :
            ].astype(BF16)
        self.one.start()

    def second(self):
        self.one.wait_recv()
        for x in range(2):
            self.q[x] = (self.p[self.core, x].astype(F32) + self.r1[x].astype(F32)).astype(BF16)
        self.two.start()

    def third(self):
        self.two.wait_recv()
        self.s[...] = (self.q[self.x].astype(F32) + self.r2[...].astype(F32)).astype(BF16)
        for copy in self.three:
            copy.start()

    def last(self, out):
        inline = self.place[0]
        total = self.q[self.x, inline].astype(F32) + self.r2[inline].astype(F32)
        for n, copy in enumerate(self.three):
            copy.wait_recv()
            total = total + self.r3[n].astype(F32)
        out[...] = total[: self.rows]

    def sent(self):
        self.one.wait_send()
        self.two.wait_send()
        for copy in self.three:
            copy.wait_send()


def spread_depth(padded, wide, turned, shape):
    rows, cols, depth = shape
    for pi in range(rows + 2):
        cells = padded[pi].astype(F32)
        edge = jnp.zeros((cols + 2, 1, LANES), F32)
        before = jnp.concatenate([edge, cells[:, : depth - 1]], axis=1)
        after = jnp.concatenate([cells[:, 1:], edge], axis=1)
        order = (after, cells, before) if turned else (before, cells, after)
        for c in range(3):
            wide[pi, :, :, c * LANES : (c + 1) * LANES] = order[c].astype(BF16)


def kernel(
    sizes, fused,
    vol, k1, k2, cot, latent, out1, out2,
    vpad, vwide, fine, cpad, cwide, hpad, hwide, w1, w2, pre, bpre, g1, g2,
    vs, vr, cs, cr, hs, hr, w1s, w1r, w1l, w2s, w2r, w2l, *rest,
):
    inlines, xlines = sizes
    inline, xline = lax.axis_index("inline"), lax.axis_index("xline")
    place = (inline, xline, inlines, xlines)
    rows, cols, depth = cot.shape[0], cot.shape[1], cot.shape[2]
    count = cols * depth

    barrier = pltpu.get_barrier_semaphore()
    if fused:
        for di in range(inlines):
            for dx in range(xlines):
                if di or dx:
                    pl.semaphore_signal(
                        barrier, inc=1, device_id_type=MESH,
                        device_id={
                            "inline": lax.rem(inline + di, inlines),
                            "xline": lax.rem(xline + dx, xlines),
                        },
                    )
        pl.semaphore_wait(barrier, inlines * xlines - 1)
    else:
        def greet(di, first):
            for dx in range(first, xlines):
                pl.semaphore_signal(
                    barrier, inc=1, device_id_type=MESH,
                    device_id={
                        "inline": lax.rem(inline + di + inlines, inlines),
                        "xline": lax.rem(xline + dx, xlines),
                    },
                )

        greet(0, 1)
        pl.semaphore_wait(barrier, xlines - 1)
        for di, has in ((1, inline < inlines - 1), (-1, inline > 0)):
            pl.when(has)(functools.partial(greet, di, 0))
        for has in (inline < inlines - 1, inline > 0):
            @pl.when(has)
            def _():
                pl.semaphore_wait(barrier, xlines)

    volume_rim = Rim(vol, vpad, 1, vs, vr, UP_WAYS, place)
    cot_rim = Rim(cot, cpad, 1, cs, cr, ALL_WAYS, place)
    first = Spread(k1, w1, (w1s, w1r, w1l), place)
    second = Spread(k2, w2, (w2s, w2r, w2l), place)
    volume_rim.start()
    first.start()
    cot_rim.start()
    second.start()

    volume_rim.clear()
    cot_rim.clear()
    cpad[1 : rows + 1, 1 : cols + 1] = cot[...]
    fine[:, 0:8, :] = jnp.zeros((fine.shape[0], 8, LANES), F32)

    def split(plane, index, py):
        for c in range(3):
            vwide[index, py % 2, py // 2, :, c * LANES : (c + 1) * LANES] = plane[
                py, pl.ds(7 + c, depth, stride=2), :
            ].astype(BF16)

    def own_plane(index, carry):
        fine[1 : 2 * cols + 1, 8:, :] = vol[index].astype(F32)
        for py in range(1, 2 * cols + 1):
            split(fine, index + 1, py)
        return carry

    lax.fori_loop(0, 2 * rows, own_plane, 0)
    volume_rim.arrive()
    fine[0 : 2 * cols + 1, 8:, :] = vpad[0].astype(F32)
    for py in range(2 * cols + 1):
        split(fine, 0, py)
    for px in range(1, 2 * rows + 1):
        fine[px, 8:, :] = vpad[px, 0].astype(F32)
        for c in range(3):
            vwide[px, 0, 0, :, c * LANES : (c + 1) * LANES] = fine[
                px, pl.ds(7 + c, depth, stride=2), :
            ].astype(BF16)

    cot_rim.arrive()
    spread_depth(cpad, cwide, True, (rows, cols, depth))

    def fine_taps(i, a, b):
        return vwide[2 * i + a, b % 2, pl.ds(b // 2, cols)].reshape(count, 3 * LANES)

    def unit_taps(wide, i, a, b):
        return wide[i + a, pl.ds(b, cols)].reshape(count, 3 * LANES)

    steps = list(itertools.product(range(3), repeat=2))

    first.forward()
    first.arrive()
    for i in range(rows):
        total = jnp.zeros((count, LANES), F32)
        for a, b in steps:
            taps = w1[pl.ds(9 * a + 3 * b, 3)].reshape(3 * LANES, LANES)
            total = total + dot(fine_taps(i, a, b), taps)
        pre[i] = total
        hidden = (total / (1.0 + jnp.exp(-total))).astype(BF16)
        hpad[i + 1, 1 : cols + 1] = hidden.reshape(cols, depth, LANES)
    hidden_own = hpad.at[pl.ds(1, rows), pl.ds(1, cols)]
    hidden_rim = Rim(hidden_own, hpad, 1, hs, hr, ALL_WAYS, place)
    hidden_rim.start()
    hidden_rim.clear()
    second.forward()

    if fused:
        bufs, sems = rest[:12], rest[12:]
        sum2 = Scatter(g2, bufs[:6], sems[:2], place)
        sum1 = Scatter(g1, bufs[6:], sems[2:], place)
        pad = g1.shape[0] - TAPS * LANES
        for g in (g1, g2):
            g[TAPS * LANES :, :] = jnp.zeros((pad, LANES), F32)

    turned = [
        hpad[i + 1, 1 : cols + 1].reshape(count, LANES).astype(F32).T.astype(BF16)
        for i in range(rows)
    ]
    for a, b in steps:
        total = jnp.zeros((LANES, 3 * LANES), F32)
        for i in range(rows):
            total = total + dot(turned[i], unit_taps(cwide, i, 2 - a, 2 - b))
        for c in range(3):
            g2[pl.ds((9 * a + 3 * b + c) * LANES, LANES), :] = total[:, c * LANES : (c + 1) * LANES]
    if fused:
        sum2.first()

    second.arrive()
    for i in range(rows):
        total = jnp.zeros((count, LANES), F32)
        for a, b in steps:
            for c in range(3):
                cells = cwide[
                    i + 2 - a, pl.ds(2 - b, cols), :, c * LANES : (c + 1) * LANES
                ].reshape(count, LANES)
                total = total + dot(cells, w2[9 * a + 3 * b + c], ((1,), (1,)))
        value = pre[i]
        sigma = 1.0 / (1.0 + jnp.exp(-value))
        bpre[i] = (total * sigma * (1.0 + value * (1.0 - sigma))).astype(BF16)
    if fused:
        sum2.second()

    for a, b in steps:
        total = jnp.zeros((3 * LANES, LANES), F32)
        for i in range(rows):
            total = total + dot(fine_taps(i, a, b), bpre[i], ((0,), (0,)))
        g1[pl.ds((9 * a + 3 * b) * LANES, 3 * LANES), :] = total
    if fused:
        sum1.first()
        sum2.third()

    hidden_rim.arrive()
    spread_depth(hpad, hwide, False, (rows, cols, depth))
    if fused:
        sum1.second()
    for i in range(rows):
        total = jnp.zeros((count, LANES), F32)
        for a, b in steps:
            taps = w2[pl.ds(9 * a + 3 * b, 3)].reshape(3 * LANES, LANES)
            total = total + dot(unit_taps(hwide, i, a, b), taps)
        latent[i] = total.astype(BF16).reshape(cols, depth, LANES)

    if fused:
        sum1.third()
        sum2.last(out2)
        sum1.last(out1)
        sum1.sent()
        sum2.sent()
    else:
        out1[...] = g1[: TAPS * LANES]
        out2[...] = g2[: TAPS * LANES]
    for group in (volume_rim, cot_rim, hidden_rim, first, second):
        group.sent()


def local(volume, first_kernel, second_kernel, cotangent):
    inlines, xlines = lax.axis_size("inline"), lax.axis_size("xline")
    rows, cols, depth, channels = cotangent.shape
    shards = inlines * xlines
    fused = inlines <= 4 and (TAPS * LANES) % (8 * shards) == 0
    out_rows = TAPS * LANES // shards if fused else TAPS * LANES
    slot = -(-out_rows // 16) * 16
    dma = pltpu.SemaphoreType.DMA
    pad_cells = (rows + 2, cols + 2, depth)
    scratch = [
        pltpu.VMEM((2 * rows + 1, 2 * cols + 1, 2 * depth, channels), BF16),
        pltpu.VMEM((2 * rows + 1, 2, cols + 1, depth, 3 * channels), BF16),
        pltpu.VMEM((2 * cols + 1, 2 * depth + 8, channels), F32),
        pltpu.VMEM(pad_cells + (channels,), BF16),
        pltpu.VMEM(pad_cells + (3 * channels,), BF16),
        pltpu.VMEM(pad_cells + (channels,), BF16),
        pltpu.VMEM(pad_cells + (3 * channels,), BF16),
        pltpu.VMEM((TAPS, channels, channels), BF16),
        pltpu.VMEM((TAPS, channels, channels), BF16),
        pltpu.VMEM((rows, cols * depth, channels), F32),
        pltpu.VMEM((rows, cols * depth, channels), BF16),
        pltpu.VMEM((TAPS * channels + 8, channels), F32),
        pltpu.VMEM((TAPS * channels + 8, channels), F32),
        dma((3,)), dma((3,)), dma((8,)), dma((8,)), dma((8,)), dma((8,)),
        dma((3,)), dma((3,)), dma, dma((3,)), dma((3,)), dma,
    ]
    if fused:
        for _ in range(2):
            scratch += [
                pltpu.VMEM((2, 2, inlines, slot, channels), BF16),
                pltpu.VMEM((2, inlines, slot, channels), BF16),
                pltpu.VMEM((2, inlines, slot, channels), BF16),
                pltpu.VMEM((inlines, slot, channels), BF16),
                pltpu.VMEM((inlines, slot, channels), BF16),
                pltpu.VMEM((max(inlines - 1, 1), slot, channels), BF16),
            ]
        scratch += [dma((inlines + 1,))] * 4
    flops = 10 * TAPS * channels * channels * rows * cols * depth
    latent, grad1, grad2 = pl.pallas_call(
        functools.partial(kernel, (inlines, xlines), fused),
        out_shape=[
            jax.ShapeDtypeStruct(cotangent.shape, BF16),
            jax.ShapeDtypeStruct((out_rows, channels), F32),
            jax.ShapeDtypeStruct((out_rows, channels), F32),
        ],
        in_specs=[pl.BlockSpec(memory_space=pltpu.VMEM)] * 4,
        out_specs=[pl.BlockSpec(memory_space=pltpu.VMEM)] * 3,
        scratch_shapes=scratch,
        cost_estimate=pl.CostEstimate(flops=flops, bytes_accessed=4 << 20, transcendentals=0),
        compiler_params=pltpu.CompilerParams(
            collective_id=0, has_side_effects=True, vmem_limit_bytes=48 << 20
        ),
    )(volume, first_kernel, second_kernel, cotangent)
    grads = [grad1.reshape(-1), grad2.reshape(-1)]
    if not fused:
        grads = [
            lax.psum_scatter(g, ("inline", "xline"), scatter_dimension=0, tiled=True) for g in grads
        ]
    return latent, grads[0], grads[1]


def solution(mesh):
    return jax.shard_map(
        local,
        mesh=mesh,
        in_specs=(
            P(("group", "inline"), "xline", None, None),
            P(None, "xline", None),
            P(None, "xline", None),
            P(("group", "inline"), "xline", None, None),
        ),
        out_specs=(
            P(("group", "inline"), "xline", None, None),
            P(("group", "inline", "xline")),
            P(("group", "inline", "xline")),
        ),
        check_vma=False,
    )
```

```python
import functools
import itertools

import jax
import jax.numpy as jnp
from jax import lax
from jax.experimental import pallas as pl
from jax.experimental.pallas import tpu as pltpu
from jax.sharding import PartitionSpec as P

F32 = jnp.float32
BF16 = jnp.bfloat16
MESH = pl.DeviceIdType.MESH
TAPS = 27
LANES = 128
ALL_WAYS = [d for d in itertools.product((-1, 0, 1), repeat=2) if d != (0, 0)]
UP_WAYS = [(1, 0), (0, 1), (1, 1)]


def dot(left, right, dims=((1,), (0,))):
    return lax.dot_general(left, right, (dims, ((), ())), preferred_element_type=F32)


def remote(src, dst, send, recv, device):
    return pltpu.make_async_remote_copy(
        src_ref=src, dst_ref=dst, send_sem=send, recv_sem=recv,
        device_id=device, device_id_type=MESH,
    )


def beside(at, count):
    return (at + count - 2) // (count - 1) + (2 * count - 3 - at) // (count - 1)


class Rim:
    def __init__(self, own, padded, low, send, recv, ways, place):
        inline, xline, inlines, xlines = place
        rows, cols = own.shape[0], own.shape[1]
        self.padded = padded
        self.items = []
        for n, (di, dx) in enumerate(ways):
            def there(si, sx, place=place):
                ok = None
                for step, at, count in ((si, inline, inlines), (sx, xline, xlines)):
                    if step == 1:
                        one = at < count - 1
                    elif step == -1:
                        one = at > 0
                    else:
                        continue
                    ok = one if ok is None else jnp.logical_and(ok, one)
                return ok

            def source(step, count):
                return {1: pl.ds(count - 1, 1), -1: pl.ds(0, 1), 0: pl.ds(0, count)}[step]

            def target(step, count):
                return {1: pl.ds(0, 1), -1: pl.ds(low + count, 1), 0: pl.ds(low, count)}[step]

            spot = (target(di, rows), target(dx, cols))
            copy = remote(
                own.at[source(di, rows), source(dx, cols)],
                padded.at[spot[0], spot[1]],
                send.at[n],
                recv.at[n],
                {
                    "inline": lax.rem(inline + di + inlines, inlines),
                    "xline": lax.rem(xline + dx + xlines, xlines),
                },
            )
            self.items.append((copy, spot, there(di, dx), there(-di, -dx)))

    def start(self):
        for copy, _, sends, _ in self.items:
            pl.when(sends)(copy.start)

    def clear(self):
        for _, spot, _, gets in self.items:
            @pl.when(jnp.logical_not(gets))
            def _():
                shape = (spot[0].size, spot[1].size) + tuple(self.padded.shape[2:])
                self.padded[spot[0], spot[1]] = jnp.zeros(shape, self.padded.dtype)

    def arrive(self):
        for copy, _, _, gets in self.items:
            pl.when(gets)(copy.wait_recv)

    def sent(self):
        for copy, _, sends, _ in self.items:
            pl.when(sends)(copy.wait_send)


class Spread:
    def __init__(self, shard, whole, sems, place):
        _, xline, _, _ = place
        send, recv, local = sems
        width = shard.shape[1]
        near = xline + 1 - 2 * lax.rem(xline, 2)
        far = lax.rem(xline + 2, 4)

        def part(index):
            return whole.at[:, pl.ds(pl.multiple_of(index * width, width), width), :]

        self.own = pltpu.make_async_copy(shard, part(xline), local)
        self.far = remote(shard, part(xline), send.at[0], recv.at[0], {"xline": far})
        self.near = remote(shard, part(xline), send.at[1], recv.at[1], {"xline": near})
        self.pass_on = remote(part(far), part(far), send.at[2], recv.at[2], {"xline": near})

    def start(self):
        self.far.start()
        self.near.start()
        self.own.start()

    def forward(self):
        self.far.wait_recv()
        self.pass_on.start()

    def arrive(self):
        self.own.wait()
        self.near.wait_recv()
        self.pass_on.wait_recv()

    def sent(self):
        self.far.wait_send()
        self.near.wait_send()
        self.pass_on.wait_send()


class Scatter:
    def __init__(self, total, bufs, sems, place, offset, rows):
        inline, xline, inlines, _ = place
        self.total, self.place = total, place
        self.p, self.r1, self.q, self.r2, self.s, self.r3 = bufs
        send, recv = sems
        self.core, self.x = lax.rem(xline, 2), xline // 2
        near = xline + 1 - 2 * self.core
        far = lax.rem(xline + 2, 4)
        self.stride = TAPS * LANES // (4 * inlines)
        self.offset, self.rows = offset, rows
        self.one = remote(self.p.at[1 - self.core], self.r1, send.at[0], recv.at[0], {"xline": near})
        self.two = remote(self.q.at[1 - self.x], self.r2, send.at[1], recv.at[1], {"xline": far})
        self.three = []
        for d in range(1, inlines):
            to = lax.rem(inline + d, inlines)
            self.three.append(
                remote(self.s.at[to], self.r3.at[d - 1], send.at[1 + d], recv.at[1 + d], {"inline": to})
            )

    def first(self):
        slot_rows = self.p.shape[3]
        for slot in range(4 * self.place[2]):
            self.p[slot % 2, slot // 2 % 2, slot // 4] = self.total[
                pl.ds(slot * self.stride + self.offset, slot_rows), :
            ].astype(BF16)
        self.one.start()

    def second(self):
        self.one.wait_recv()
        for x in range(2):
            self.q[x] = (self.p[self.core, x].astype(F32) + self.r1[x].astype(F32)).astype(BF16)
        self.two.start()

    def third(self):
        self.two.wait_recv()
        self.s[...] = (self.q[self.x].astype(F32) + self.r2[...].astype(F32)).astype(BF16)
        for copy in self.three:
            copy.start()

    def last(self, out):
        inline = self.place[0]
        total = self.q[self.x, inline].astype(F32) + self.r2[inline].astype(F32)
        for n, copy in enumerate(self.three):
            copy.wait_recv()
            total = total + self.r3[n].astype(F32)
        out[pl.ds(self.offset, self.rows), :] = total[: self.rows]

    def sent(self):
        self.one.wait_send()
        self.two.wait_send()
        for copy in self.three:
            copy.wait_send()


def chunks_of(rows):
    half = -(-rows // 32) * 16
    return [(0, half), (half, rows - half)] if half < rows else [(0, rows)]


def spread_depth(padded, wide, turned, shape):
    rows, cols, depth = shape
    for pi in range(rows + 2):
        cells = padded[pi].astype(F32)
        edge = jnp.zeros((cols + 2, 1, LANES), F32)
        before = jnp.concatenate([edge, cells[:, : depth - 1]], axis=1)
        after = jnp.concatenate([cells[:, 1:], edge], axis=1)
        order = (after, cells, before) if turned else (before, cells, after)
        for c in range(3):
            wide[pi, :, :, c * LANES : (c + 1) * LANES] = order[c].astype(BF16)


def kernel(
    sizes, fused,
    vol_hbm, k1_hbm, k2_hbm, cot_hbm, latent, out1, out2, vol, k1, k2, cot, load,
    vpad, vwide, fine, cpad, cwide, hpad, hwide, w1, w2, pre, bpre, g1, g2,
    vs, vr, cs, cr, hs, hr, w1s, w1r, w1l, w2s, w2r, w2l, *rest,
):
    inlines, xlines = sizes
    inline, xline = lax.axis_index("inline"), lax.axis_index("xline")
    place = (inline, xline, inlines, xlines)
    rows, cols, depth = cot.shape[0], cot.shape[1], cot.shape[2]
    count = cols * depth

    loads = [
        pltpu.make_async_copy(src, dst, load.at[n])
        for n, (src, dst) in enumerate(
            ((vol_hbm, vol), (k1_hbm, k1), (cot_hbm, cot), (k2_hbm, k2))
        )
    ]
    for copy in loads:
        copy.start()

    barrier = pltpu.get_barrier_semaphore()
    if fused:
        def hello(di, dx):
            pl.semaphore_signal(
                barrier, inc=1, device_id_type=MESH,
                device_id={
                    "inline": lax.rem(inline + di + inlines, inlines),
                    "xline": lax.rem(xline + dx + xlines, xlines),
                },
            )

        corners = [
            (
                di, dx,
                jnp.logical_and(
                    inline < inlines - 1 if di > 0 else inline > 0,
                    xline < xlines - 1 if dx > 0 else xline > 0,
                ),
            )
            for di, dx in ALL_WAYS if di and dx
        ]
        for di in range(1, inlines):
            hello(di, 0)
        for dx in range(1, xlines):
            hello(0, dx)
        for di, dx, has in corners:
            pl.when(has)(functools.partial(hello, di, dx))
        pl.semaphore_wait(
            barrier, inlines + xlines - 2 + beside(inline, inlines) * beside(xline, xlines)
        )
    else:
        def greet(di, first):
            for dx in range(first, xlines):
                pl.semaphore_signal(
                    barrier, inc=1, device_id_type=MESH,
                    device_id={
                        "inline": lax.rem(inline + di + inlines, inlines),
                        "xline": lax.rem(xline + dx, xlines),
                    },
                )

        greet(0, 1)
        for di, has in ((1, inline < inlines - 1), (-1, inline > 0)):
            pl.when(has)(functools.partial(greet, di, 0))
        pl.semaphore_wait(barrier, xlines - 1 + xlines * beside(inline, inlines))

    volume_rim = Rim(vol, vpad, 1, vs, vr, UP_WAYS, place)
    cot_rim = Rim(cot, cpad, 1, cs, cr, ALL_WAYS, place)
    first = Spread(k1, w1, (w1s, w1r, w1l), place)
    second = Spread(k2, w2, (w2s, w2r, w2l), place)
    for copy, group in zip(loads, (volume_rim, first, cot_rim, second)):
        copy.wait()
        group.start()

    volume_rim.clear()
    cot_rim.clear()
    cpad[1 : rows + 1, 1 : cols + 1] = cot[...]
    fine[:, 0:8, :] = jnp.zeros((fine.shape[0], 8, LANES), F32)

    def split(plane, index, py):
        for c in range(3):
            vwide[index, py % 2, py // 2, :, c * LANES : (c + 1) * LANES] = plane[
                py, pl.ds(7 + c, depth, stride=2), :
            ].astype(BF16)

    def own_plane(index, carry):
        fine[1 : 2 * cols + 1, 8:, :] = vol[index].astype(F32)
        for py in range(1, 2 * cols + 1):
            split(fine, index + 1, py)
        return carry

    lax.fori_loop(0, 2 * rows, own_plane, 0)
    volume_rim.arrive()
    fine[0 : 2 * cols + 1, 8:, :] = vpad[0].astype(F32)
    for py in range(2 * cols + 1):
        split(fine, 0, py)
    for px in range(1, 2 * rows + 1):
        fine[px, 8:, :] = vpad[px, 0].astype(F32)
        for c in range(3):
            vwide[px, 0, 0, :, c * LANES : (c + 1) * LANES] = fine[
                px, pl.ds(7 + c, depth, stride=2), :
            ].astype(BF16)

    cot_rim.arrive()
    spread_depth(cpad, cwide, True, (rows, cols, depth))

    def fine_taps(i, a, b):
        return vwide[2 * i + a, b % 2, pl.ds(b // 2, cols)].reshape(count, 3 * LANES)

    def unit_taps(wide, i, a, b):
        return wide[i + a, pl.ds(b, cols)].reshape(count, 3 * LANES)

    steps = list(itertools.product(range(3), repeat=2))

    first.forward()
    first.arrive()
    for i in range(rows):
        total = jnp.zeros((count, LANES), F32)
        for a, b in steps:
            taps = w1[pl.ds(9 * a + 3 * b, 3)].reshape(3 * LANES, LANES)
            total = total + dot(fine_taps(i, a, b), taps)
        pre[i] = total
        hidden = (total / (1.0 + jnp.exp(-total))).astype(BF16)
        hpad[i + 1, 1 : cols + 1] = hidden.reshape(cols, depth, LANES)
    hidden_own = hpad.at[pl.ds(1, rows), pl.ds(1, cols)]
    hidden_rim = Rim(hidden_own, hpad, 1, hs, hr, ALL_WAYS, place)
    hidden_rim.start()
    hidden_rim.clear()
    second.forward()

    if fused:
        parts = chunks_of(TAPS * LANES // (inlines * xlines))
        cut = len(parts)
        bufs, sems = rest[: 12 * cut], rest[12 * cut :]
        sums = [
            Scatter(
                (g2, g1)[n // cut], bufs[6 * n : 6 * n + 6], sems[2 * n : 2 * n + 2], place,
                *parts[n % cut],
            )
            for n in range(2 * cut)
        ]
        sum2, sum1 = sums[:cut], sums[cut:]
        pad = g1.shape[0] - TAPS * LANES
        for g in (g1, g2):
            g[TAPS * LANES :, :] = jnp.zeros((pad, LANES), F32)

    turned = [
        hpad[i + 1, 1 : cols + 1].reshape(count, LANES).astype(F32).T.astype(BF16)
        for i in range(rows)
    ]
    for a, b in steps:
        total = jnp.zeros((LANES, 3 * LANES), F32)
        for i in range(rows):
            total = total + dot(turned[i], unit_taps(cwide, i, 2 - a, 2 - b))
        for c in range(3):
            g2[pl.ds((9 * a + 3 * b + c) * LANES, LANES), :] = total[:, c * LANES : (c + 1) * LANES]
    if fused:
        for part in sum2:
            part.first()

    second.arrive()
    for i in range(rows):
        total = jnp.zeros((count, LANES), F32)
        for a, b in steps:
            for c in range(3):
                cells = cwide[
                    i + 2 - a, pl.ds(2 - b, cols), :, c * LANES : (c + 1) * LANES
                ].reshape(count, LANES)
                total = total + dot(cells, w2[9 * a + 3 * b + c], ((1,), (1,)))
        value = pre[i]
        sigma = 1.0 / (1.0 + jnp.exp(-value))
        bpre[i] = (total * sigma * (1.0 + value * (1.0 - sigma))).astype(BF16)
    if fused:
        for part in sum2:
            part.second()

    for a, b in steps:
        total = jnp.zeros((3 * LANES, LANES), F32)
        for i in range(rows):
            total = total + dot(fine_taps(i, a, b), bpre[i], ((0,), (0,)))
        g1[pl.ds((9 * a + 3 * b) * LANES, 3 * LANES), :] = total
    if fused:
        for part in sum1:
            part.first()
        for part in sum2:
            part.third()

    hidden_rim.arrive()
    spread_depth(hpad, hwide, False, (rows, cols, depth))
    if fused:
        for part in sum1:
            part.second()
    for i in range(rows):
        total = jnp.zeros((count, LANES), F32)
        for a, b in steps:
            taps = w2[pl.ds(9 * a + 3 * b, 3)].reshape(3 * LANES, LANES)
            total = total + dot(unit_taps(hwide, i, a, b), taps)
        latent[i] = total.astype(BF16).reshape(cols, depth, LANES)

    if fused:
        for part in sum1:
            part.third()
        for part in sum2:
            part.last(out2)
        for part in sum1:
            part.last(out1)
        for part in sum1:
            part.sent()
        for part in sum2:
            part.sent()
    else:
        out1[...] = g1[: TAPS * LANES]
        out2[...] = g2[: TAPS * LANES]
    for group in (volume_rim, cot_rim, hidden_rim, first, second):
        group.sent()


def local(volume, first_kernel, second_kernel, cotangent):
    inlines, xlines = lax.axis_size("inline"), lax.axis_size("xline")
    rows, cols, depth, channels = cotangent.shape
    shards = inlines * xlines
    fused = inlines <= 4 and (TAPS * LANES) % (8 * shards) == 0
    out_rows = TAPS * LANES // shards if fused else TAPS * LANES
    dma = pltpu.SemaphoreType.DMA
    pad_cells = (rows + 2, cols + 2, depth)
    scratch = [
        pltpu.VMEM(volume.shape, BF16),
        pltpu.VMEM(first_kernel.shape, BF16),
        pltpu.VMEM(second_kernel.shape, BF16),
        pltpu.VMEM(cotangent.shape, BF16),
        dma((4,)),
        pltpu.VMEM((2 * rows + 1, 2 * cols + 1, 2 * depth, channels), BF16),
        pltpu.VMEM((2 * rows + 1, 2, cols + 1, depth, 3 * channels), BF16),
        pltpu.VMEM((2 * cols + 1, 2 * depth + 8, channels), F32),
        pltpu.VMEM(pad_cells + (channels,), BF16),
        pltpu.VMEM(pad_cells + (3 * channels,), BF16),
        pltpu.VMEM(pad_cells + (channels,), BF16),
        pltpu.VMEM(pad_cells + (3 * channels,), BF16),
        pltpu.VMEM((TAPS, channels, channels), BF16),
        pltpu.VMEM((TAPS, channels, channels), BF16),
        pltpu.VMEM((rows, cols * depth, channels), F32),
        pltpu.VMEM((rows, cols * depth, channels), BF16),
        pltpu.VMEM((TAPS * channels + 8, channels), F32),
        pltpu.VMEM((TAPS * channels + 8, channels), F32),
        dma((3,)), dma((3,)), dma((8,)), dma((8,)), dma((8,)), dma((8,)),
        dma((3,)), dma((3,)), dma, dma((3,)), dma((3,)), dma,
    ]
    if fused:
        for _, chunk in chunks_of(out_rows) * 2:
            slot = -(-chunk // 16) * 16
            scratch += [
                pltpu.VMEM((2, 2, inlines, slot, channels), BF16),
                pltpu.VMEM((2, inlines, slot, channels), BF16),
                pltpu.VMEM((2, inlines, slot, channels), BF16),
                pltpu.VMEM((inlines, slot, channels), BF16),
                pltpu.VMEM((inlines, slot, channels), BF16),
                pltpu.VMEM((max(inlines - 1, 1), slot, channels), BF16),
            ]
        scratch += [dma((inlines + 1,))] * (4 * len(chunks_of(out_rows)))
    flops = 10 * TAPS * channels * channels * rows * cols * depth
    latent, grad1, grad2 = pl.pallas_call(
        functools.partial(kernel, (inlines, xlines), fused),
        out_shape=[
            jax.ShapeDtypeStruct(cotangent.shape, BF16),
            jax.ShapeDtypeStruct((out_rows, channels), F32),
            jax.ShapeDtypeStruct((out_rows, channels), F32),
        ],
        in_specs=[pl.BlockSpec(memory_space=pltpu.HBM)] * 4,
        out_specs=[pl.BlockSpec(memory_space=pltpu.VMEM)] * 3,
        scratch_shapes=scratch,
        cost_estimate=pl.CostEstimate(flops=flops, bytes_accessed=4 << 20, transcendentals=0),
        compiler_params=pltpu.CompilerParams(
            collective_id=0, has_side_effects=True, vmem_limit_bytes=48 << 20
        ),
    )(volume, first_kernel, second_kernel, cotangent)
    grads = [grad1.reshape(-1), grad2.reshape(-1)]
    if not fused:
        grads = [
            lax.psum_scatter(g, ("inline", "xline"), scatter_dimension=0, tiled=True) for g in grads
        ]
    return latent, grads[0], grads[1]


def solution(mesh):
    return jax.shard_map(
        local,
        mesh=mesh,
        in_specs=(
            P(("group", "inline"), "xline", None, None),
            P(None, "xline", None),
            P(None, "xline", None),
            P(("group", "inline"), "xline", None, None),
        ),
        out_specs=(
            P(("group", "inline"), "xline", None, None),
            P(("group", "inline", "xline")),
            P(("group", "inline", "xline")),
        ),
        check_vma=False,
    )
```
